32 devices in a mesh: section: 16 (over z, y, x), tensor: 2 (over core).
Axes of the slice: x: 2, y: 2, z: 4, core: 2. Of those that a mesh axis runs over, the one named last changes fastest.
Arguments:
- section_norm_gain: float32 [16, 4096], P('section'), may hold values from 0.5 to 1.5
- query_weight_matrix: bfloat16 [16, 4096, 4096], P('section', None, 'tensor'), may hold values from -2 to 2
- key_weight_matrix: bfloat16 [16, 4096, 1024], P('section', None, 'tensor'), may hold values from -2 to 2
- value_weight_matrix: bfloat16 [16, 4096, 1024], P('section', None, 'tensor'), may hold values from -0.09375 to 0.09375
- output_weight_matrix: bfloat16 [16, 4096, 4096], P('section', 'tensor'), may hold values from -0.09375 to 0.09375
- adapter_down_weight: bfloat16 [16, 2, 8, 4096], P('section'), may hold values from -0.09375 to 0.09375
- query_up_weight: bfloat16 [16, 8, 4096], P('section', None, 'tensor'), may hold values from -2 to 2
- value_up_weight: bfloat16 [16, 8, 1024], P('section', None, 'tensor'), may hold values from -2 to 2
- arriving: bfloat16 [16, 128, 4096], P('section', None, 'tensor'), may hold values from -6 to 6
- entering: bfloat16 [1, 128, 4096], P(None, None, 'tensor'), may hold values from -6 to 6
- returning: bfloat16 [16, 128, 4096], P('section', None, 'tensor'), may hold values from -6 to 6
- loss_head_gradient: bfloat16 [1, 128, 4096], P(None, None, 'tensor'), may hold values from -6 to 6
- parked: bfloat16 [16, 2, 128, 4096], P('section', None, None, 'tensor'), may hold values from -6 to 6
- forward_document_ids: int32 [17, 128], replicated, may hold values from 0 to 3, never falling along the last dimension, each value on 1 to 64 neighbouring positions
- backward_document_ids: int32 [17, 128], replicated, may hold values from 0 to 3, never falling along the last dimension, each value on 1 to 64 neighbouring positions
Outputs:
- departing: bfloat16 [16, 128, 4096], P('section', None, 'tensor')
- returned: bfloat16 [16, 128, 4096], P('section', None, 'tensor')
- parked_out: bfloat16 [16, 2, 128, 4096], P('section', None, None, 'tensor')
- grad_down: float32 [16, 2, 8, 4096], P('section', None, None, 'tensor')
- grad_up_query: float32 [16, 8, 4096], P('section', None, 'tensor')
- grad_up_value: float32 [16, 8, 1024], P('section', None, 'tensor')
The draws below stay inside these ranges and needn't reach their ends.
Inputs may be any that keep to these rules, and one draw needn't show every extreme that they name: `forward_document_ids`: document ids never fall along a row; each of the 4 documents of a micro-batch holds 1 to 64 positions. `backward_document_ids`: document ids never fall along a row; each of the 4 documents of a micro-batch holds 1 to 64 positions.
All inputs are finite; a program needn't handle non-finite values.
Results may differ from the reference program's by a relative error of at most 0.024.
The reference program's roundings to bfloat16 on the way count: a program that leaves them out, or rounds other values in their place, can miss the bound.
Values may be sent and summed in bfloat16 or wider, within the bound.
A program may use at most 192 MiB of HBM per device.

```python
import math
import jax
import jax.numpy as jnp
import numpy as np
from jax import lax

MODEL_WIDTH = 4096
HEADS = 32
KV_HEADS = 8
HEAD = 128
ADAPTER_RANK = 8
ROWS = 128
TICKS = 2
DOCS = 4
MICRO = 17
N_SECTION = 16


def draw_query_weight_matrix(key, part):
    own_key = jax.random.fold_in(key, 11)
    columns = HEADS * HEAD
    drawn = jax.random.truncated_normal(own_key, -6.0, 6.0, (N_SECTION, MODEL_WIDTH, columns), jnp.float32) / math.sqrt(MODEL_WIDTH)
    return drawn.astype(jnp.bfloat16)


def draw_key_weight_matrix(key, part):
    own_key = jax.random.fold_in(key, 12)
    columns = KV_HEADS * HEAD
    drawn = jax.random.truncated_normal(own_key, -6.0, 6.0, (N_SECTION, MODEL_WIDTH, columns), jnp.float32) / math.sqrt(MODEL_WIDTH)
    return drawn.astype(jnp.bfloat16)


def level_of(key, dims, cuts, least, high):
    def one(axis_at, shards_of):
        draws = jax.random.uniform(jax.random.fold_in(jax.random.fold_in(key, 6), axis_at), (shards_of,), jnp.float32, least / len(cuts), high / len(cuts))
        return jnp.repeat(jnp.exp(draws), dims[axis_at] // shards_of).reshape((-1,) + (1,) * (len(dims) - axis_at - 1))

    level = one(*cuts[0])
    for cut in cuts[1:]:
        level = level * one(*cut)
    return level


def split_up(number_of, total, reach, lean):
    loads = [(1 << 20) // math.isqrt(rank ** lean) + 1 for rank in range(2, number_of + 1)]
    spare, holding = total - reach - (number_of - 1), [1] * (number_of - 1)
    while spare > 0:
        movable = [i for i in range(number_of - 1) if holding[i] < reach]
        mass, remaining = sum([loads[i] for i in movable]), spare
        for i in movable:
            more = min(reach - holding[i], max(1, remaining * loads[i] // mass), spare)
            holding[i] = holding[i] + more
            spare = spare - more
    return np.array([reach] + holding)


def ragged_sizes(key, count, total, bound, slope):
    if count == 2:
        one = jax.random.randint(key, (), max(1, total - bound), min(bound, total - 1) + 1)
        return jnp.stack([one, total - one])
    sizes = jnp.asarray(split_up(count, total, bound, slope), jnp.int32)
    couples = (count - 1) // 2
    donor, receiver = sizes[1:1 + 2 * couples:2], sizes[2:2 + 2 * couples:2]
    slack = jnp.minimum(donor - 1, bound - receiver)
    moved = jax.random.randint(jax.random.fold_in(key, 1), (couples,), 0, 1 << 20) % (slack + 1)
    sizes = sizes.at[1:1 + 2 * couples:2].set(donor - moved).at[2:2 + 2 * couples:2].set(receiver + moved)
    return sizes[jax.random.permutation(jax.random.fold_in(key, 2), count)]


def centred(stream_key, extent, scale, most, pieces=(), kind=jnp.bfloat16):
    result = jax.random.normal(stream_key, extent, jnp.float32) * scale
    if len(pieces) > 0:
        result = level_of(stream_key, extent, pieces, -0.22, 0.18) * result
    return jnp.clip(result, min=-most, max=most).astype(kind)


def setup_inputs(seed: int = 0) -> dict:
    key_of = jax.random.split(jax.random.key(seed), 16)
    section_norm_gain = jnp.clip(1.0 + 0.1 * jax.random.normal(key_of[0], (N_SECTION, MODEL_WIDTH), jnp.float32), 0.5, 1.5)
    query_weight_matrix = draw_query_weight_matrix(jax.random.fold_in(key_of[15], 71), 0)
    key_weight_matrix = draw_key_weight_matrix(jax.random.fold_in(key_of[15], 71), 0)
    value_weight_matrix = centred(key_of[3], (N_SECTION, MODEL_WIDTH, KV_HEADS * HEAD), MODEL_WIDTH ** -0.5, 0.09375, ((0, 16), (2, 2)))
    output_weight_matrix = centred(key_of[4], (N_SECTION, HEADS * HEAD, MODEL_WIDTH), (HEADS * HEAD) ** -0.5, 0.09375, ((0, 16), (1, 2)))
    adapter_down_weight = centred(key_of[5], (N_SECTION, 2, ADAPTER_RANK, MODEL_WIDTH), MODEL_WIDTH ** -0.5, 0.09375, ((0, 16),))
    query_up_weight = centred(key_of[6], (N_SECTION, ADAPTER_RANK, HEADS * HEAD), ADAPTER_RANK ** -0.5, 2.0, ((0, 16), (2, 2)))
    value_up_weight = centred(key_of[7], (N_SECTION, ADAPTER_RANK, KV_HEADS * HEAD), ADAPTER_RANK ** -0.5, 2.0, ((0, 16), (2, 2)))
    arriving = centred(key_of[8], (N_SECTION, ROWS, MODEL_WIDTH), 1.0, 6.0, ((0, 16), (2, 2)))
    entering = centred(key_of[9], (TICKS - 1, ROWS, MODEL_WIDTH), 1.0, 6.0, ((2, 2),))
    returning = centred(key_of[10], (N_SECTION, ROWS, MODEL_WIDTH), 1.0, 6.0, ((0, 16), (2, 2)))
    loss_head_gradient = centred(key_of[11], (TICKS - 1, ROWS, MODEL_WIDTH), 1.0, 6.0, ((2, 2),))
    parked = centred(key_of[12], (N_SECTION, TICKS, ROWS, MODEL_WIDTH), 1.0, 6.0, ((0, 16), (3, 2)))
    forward_document_ids = jax.vmap(lambda own: jnp.searchsorted(jnp.cumsum(ragged_sizes(own, DOCS, ROWS, ROWS // 2, 0)), jnp.arange(ROWS), side="right"))(jax.random.split(key_of[13], MICRO)).reshape((MICRO, ROWS)).astype(jnp.int32)
    backward_document_ids = jax.vmap(lambda own: jnp.searchsorted(jnp.cumsum(ragged_sizes(own, DOCS, ROWS, ROWS // 2, 0)), jnp.arange(ROWS), side="right"))(jax.random.split(key_of[14], MICRO)).reshape((MICRO, ROWS)).astype(jnp.int32)
    return {"section_norm_gain": section_norm_gain, "query_weight_matrix": query_weight_matrix, "key_weight_matrix": key_weight_matrix, "value_weight_matrix": value_weight_matrix, "output_weight_matrix": output_weight_matrix, "adapter_down_weight": adapter_down_weight, "query_up_weight": query_up_weight, "value_up_weight": value_up_weight, "arriving": arriving, "entering": entering, "returning": returning, "loss_head_gradient": loss_head_gradient, "parked": parked, "forward_document_ids": forward_document_ids, "backward_document_ids": backward_document_ids}


eps = 1e-05
rope_base = 500000.0
mask_fill = -1e+30

def rope_tables(row_count, head_size):
    half_size = head_size // 2
    exponent = jnp.arange(half_size, dtype=jnp.float32) * (2.0 / head_size)
    frequency = jnp.exp(-exponent * math.log(rope_base))
    angles = jnp.arange(row_count, dtype=jnp.float32)[:, None] * frequency[None, :]
    return (jnp.cos(angles), jnp.sin(angles))

def rotate(value_rows_block, cosine_lookup, sine_lookup, direction):
    half_size = value_rows_block.shape[-1] // 2
    first_half = value_rows_block[..., :half_size]
    second = value_rows_block[..., half_size:]
    target_shape = (cosine_lookup.shape[0],) + (1,) * (value_rows_block.ndim - 2) + (half_size,)
    cosines = cosine_lookup.reshape(target_shape)
    sines = sine_lookup.reshape(target_shape) * direction
    return jnp.concatenate([first_half * cosines - second * sines, second * cosines + first_half * sines], axis=-1)

def apply_projection(section_inputs, norm_gain_vector, query_weight_matrix, key_weight_matrix, value_weight_matrix, adapter_down_weight, query_up_weight, value_up_weight, cosine_lookup, sine_lookup):
    adapter_rank_size = query_up_weight.shape[0]
    head_size = cosine_lookup.shape[1] * 2
    row_count = section_inputs.shape[0]
    groups = key_weight_matrix.shape[1] // head_size
    per_group = query_weight_matrix.shape[1] // head_size // groups
    inputs_single_float = section_inputs.astype(jnp.float32)
    inverse_root_mean = lax.rsqrt(lax.optimization_barrier(jnp.mean(inputs_single_float * inputs_single_float, axis=1, keepdims=True)) + eps)
    normalized_input = (inputs_single_float * inverse_root_mean * norm_gain_vector[None, :]).astype(jnp.bfloat16)
    flattened_down = adapter_down_weight.reshape(2 * adapter_rank_size, adapter_down_weight.shape[-1])
    low_rank_output = lax.dot_general(normalized_input, flattened_down, (((1,), (1,)), ((), ())), preferred_element_type=jnp.float32).astype(jnp.bfloat16)
    query_rows_block = jnp.dot(normalized_input, query_weight_matrix, preferred_element_type=jnp.float32) + jnp.dot(low_rank_output[:, :adapter_rank_size], query_up_weight, preferred_element_type=jnp.float32)
    key_row_block = jnp.dot(normalized_input, key_weight_matrix, preferred_element_type=jnp.float32)
    value_rows_block = jnp.dot(normalized_input, value_weight_matrix, preferred_element_type=jnp.float32) + jnp.dot(low_rank_output[:, adapter_rank_size:], value_up_weight, preferred_element_type=jnp.float32)
    query_rows_block = rotate(query_rows_block.reshape(row_count, groups, per_group, head_size), cosine_lookup, sine_lookup, 1.0).astype(jnp.bfloat16)
    key_row_block = rotate(key_row_block.reshape(row_count, groups, head_size), cosine_lookup, sine_lookup, 1.0).astype(jnp.bfloat16)
    value_rows_block = value_rows_block.reshape(row_count, groups, head_size).astype(jnp.bfloat16)
    return (inputs_single_float, inverse_root_mean, normalized_input, low_rank_output, query_rows_block, key_row_block, value_rows_block)

def allowed_pairs(document_list):
    positions = jnp.arange(document_list.shape[0], dtype=jnp.int32)
    return (positions[None, :] <= positions[:, None]) & (document_list[:, None] == document_list[None, :])

def attend(query_rows_block, key_row_block, value_rows_block, allowed):
    inverse = 1.0 / math.sqrt(query_rows_block.shape[-1])
    scores = jnp.einsum('qgd,kd->gqk', query_rows_block.astype(jnp.float32), key_row_block.astype(jnp.float32), precision=lax.Precision.HIGHEST) * inverse
    scores = jnp.where(allowed[None, :, :], scores, mask_fill)
    row_max = lax.optimization_barrier(jnp.max(scores, axis=2, keepdims=True))
    weights = jnp.exp(scores - row_max)
    probabilities = weights / lax.optimization_barrier(jnp.sum(weights, axis=2, keepdims=True))
    rounded = probabilities.astype(jnp.bfloat16)
    context = jnp.einsum('gqk,kd->qgd', rounded.astype(jnp.float32), value_rows_block.astype(jnp.float32), precision=lax.Precision.HIGHEST)
    return (probabilities, rounded, context)

def attend_back(query_rows_block, key_row_block, value_rows_block, probabilities, rounded, d_context):
    inverse = 1.0 / math.sqrt(query_rows_block.shape[-1])
    context_grad = d_context.astype(jnp.float32)
    d_probs = jnp.einsum('qgd,kd->gqk', context_grad, value_rows_block.astype(jnp.float32), precision=lax.Precision.HIGHEST)
    d_values = jnp.einsum('gqk,qgd->kd', rounded.astype(jnp.float32), context_grad, precision=lax.Precision.HIGHEST)
    d_score = probabilities * (d_probs - lax.optimization_barrier(jnp.sum(d_probs * probabilities, axis=2, keepdims=True))) * inverse
    score_grad = d_score.astype(jnp.bfloat16).astype(jnp.float32)
    d_queries = jnp.einsum('gqk,kd->qgd', score_grad, key_row_block.astype(jnp.float32), precision=lax.Precision.HIGHEST)
    d_keys = jnp.einsum('gqk,qgd->kd', score_grad, query_rows_block.astype(jnp.float32), precision=lax.Precision.HIGHEST)
    return (d_queries, d_keys, d_values)

def section_loss_term(section_inputs, norm_gain_vector, query_weight_matrix, key_weight_matrix, value_weight_matrix, output_weight_matrix, adapter_down_weight, query_up_weight, value_up_weight, document_list, cosine_lookup, sine_lookup):
    partial_pieces = apply_projection(section_inputs, norm_gain_vector, query_weight_matrix, key_weight_matrix, value_weight_matrix, adapter_down_weight, query_up_weight, value_up_weight, cosine_lookup, sine_lookup)
    allowed = allowed_pairs(document_list)
    probabilities, rounded, context = jax.vmap(attend, in_axes=(1, 1, 1, None), out_axes=(0, 0, 1))(partial_pieces[4], partial_pieces[5], partial_pieces[6], allowed)
    context = context.reshape(section_inputs.shape[0], -1).astype(jnp.bfloat16)
    return jnp.dot(context, output_weight_matrix, preferred_element_type=jnp.float32)

def section_backward_pass(section_inputs, incoming_cotangent, norm_gain_vector, query_weight_matrix, key_weight_matrix, value_weight_matrix, output_weight_matrix, adapter_down_weight, query_up_weight, value_up_weight, document_list, cosine_lookup, sine_lookup):
    inputs_single_float, inverse_root_mean, normalized_input, low_rank_output, query_rows_block, key_row_block, value_rows_block = apply_projection(section_inputs, norm_gain_vector, query_weight_matrix, key_weight_matrix, value_weight_matrix, adapter_down_weight, query_up_weight, value_up_weight, cosine_lookup, sine_lookup)
    adapter_rank_size = query_up_weight.shape[0]
    row_count = section_inputs.shape[0]
    allowed = allowed_pairs(document_list)
    probabilities, rounded, context = jax.vmap(attend, in_axes=(1, 1, 1, None), out_axes=(0, 0, 1))(query_rows_block, key_row_block, value_rows_block, allowed)
    last_dims = (((1,), (1,)), ((), ()))
    leading_dimensions = (((0,), (0,)), ((), ()))
    d_context = lax.dot_general(incoming_cotangent, output_weight_matrix, last_dims, preferred_element_type=jnp.float32).astype(jnp.bfloat16).reshape(query_rows_block.shape)
    d_queries, d_keys, d_values = jax.vmap(attend_back, in_axes=(1, 1, 1, 0, 0, 1), out_axes=(1, 1, 1))(query_rows_block, key_row_block, value_rows_block, probabilities, rounded, d_context)
    query_grad = rotate(d_queries, cosine_lookup, sine_lookup, -1.0).astype(jnp.bfloat16).reshape(row_count, -1)
    key_grad = rotate(d_keys, cosine_lookup, sine_lookup, -1.0).astype(jnp.bfloat16).reshape(row_count, -1)
    value_grad = d_values.astype(jnp.bfloat16).reshape(row_count, -1)
    low_rank_gradient = jnp.concatenate([lax.dot_general(query_grad, query_up_weight, last_dims, preferred_element_type=jnp.float32), lax.dot_general(value_grad, value_up_weight, last_dims, preferred_element_type=jnp.float32)], axis=1).astype(jnp.bfloat16)
    flattened_down = adapter_down_weight.reshape(2 * adapter_rank_size, adapter_down_weight.shape[-1])
    d_normed = lax.dot_general(query_grad, query_weight_matrix, last_dims, preferred_element_type=jnp.float32)
    d_normed = d_normed + lax.dot_general(key_grad, key_weight_matrix, last_dims, preferred_element_type=jnp.float32)
    d_normed = d_normed + lax.dot_general(value_grad, value_weight_matrix, last_dims, preferred_element_type=jnp.float32)
    d_normed = d_normed + jnp.dot(low_rank_gradient, flattened_down, preferred_element_type=jnp.float32)
    weighted = d_normed * norm_gain_vector[None, :]
    d_inputs = inverse_root_mean * weighted - inputs_single_float * inverse_root_mean ** 3 * lax.optimization_barrier(jnp.mean(inputs_single_float * weighted, axis=1, keepdims=True))
    down_gradient = lax.dot_general(low_rank_gradient, normalized_input, leading_dimensions, preferred_element_type=jnp.float32).reshape(adapter_down_weight.shape)
    up_query_grad = lax.dot_general(low_rank_output[:, :adapter_rank_size], query_grad, leading_dimensions, preferred_element_type=jnp.float32)
    up_value_grad = lax.dot_general(low_rank_output[:, adapter_rank_size:], value_grad, leading_dimensions, preferred_element_type=jnp.float32)
    return (d_inputs, down_gradient, up_query_grad, up_value_grad)

def reference(section_norm_gain, query_weight_matrix, key_weight_matrix, value_weight_matrix, output_weight_matrix, adapter_down_weight, query_up_weight, value_up_weight, arriving, entering, returning, loss_head_gradient, parked, forward_document_ids, backward_document_ids):
    section_count = N_SECTION
    cosine_lookup, sine_lookup = rope_tables(ROWS, HEAD)
    section_order = jnp.arange(section_count, dtype=jnp.int32)
    partner = jnp.bitwise_xor(section_order, section_count // 2)
    layer_stack = (section_norm_gain, query_weight_matrix, key_weight_matrix, value_weight_matrix, output_weight_matrix, adapter_down_weight, query_up_weight, value_up_weight)

    def forward_one(packed_item):
        section_inputs, document_list, norm_gain_vector, query_proj, key_proj, value_proj, out_proj, down_projected, up_queries, up_values = packed_item
        partial_value = section_loss_term(section_inputs, norm_gain_vector, query_proj, key_proj, value_proj, out_proj, down_projected, up_queries, up_values, document_list, cosine_lookup, sine_lookup)
        return (section_inputs.astype(jnp.float32) + partial_value).astype(jnp.bfloat16)

    def backward_one(packed_item):
        section_inputs, incoming_cotangent, document_list, norm_gain_vector, query_proj, key_proj, value_proj, out_proj, down_projected, up_queries, up_values = packed_item
        partial_value, down_gradient, up_query_grad, up_value_grad = section_backward_pass(section_inputs, incoming_cotangent, norm_gain_vector, query_proj, key_proj, value_proj, out_proj, down_projected, up_queries, up_values, document_list, cosine_lookup, sine_lookup)
        return ((incoming_cotangent.astype(jnp.float32) + partial_value).astype(jnp.bfloat16), down_gradient, up_query_grad, up_value_grad)
    held_rows = arriving
    stashed = []
    outputs = arriving
    for moment in range(TICKS):
        if moment > 0:
            held_rows = jnp.concatenate([entering[moment - 1][None], outputs[:-1]], axis=0)
        stashed.append(held_rows)
        document_list = forward_document_ids[moment - section_order + section_count - 1]
        outputs = lax.map(forward_one, (held_rows, document_list) + layer_stack)
    parked_out = jnp.stack(stashed, axis=1)[partner]
    stored = parked[partner]
    cotangents = returning
    backward_rows = returning
    down_gradient_sum = jnp.zeros(adapter_down_weight.shape, jnp.float32)
    query_total = jnp.zeros(query_up_weight.shape, jnp.float32)
    value_total = jnp.zeros(value_up_weight.shape, jnp.float32)
    for moment in range(TICKS):
        if moment > 0:
            cotangents = jnp.concatenate([backward_rows[1:], loss_head_gradient[moment - 1][None]], axis=0)
        document_list = backward_document_ids[section_order + moment]
        backward_rows, down_gradient, up_query_grad, up_value_grad = lax.map(backward_one, (stored[:, moment], cotangents, document_list) + layer_stack)
        down_gradient_sum = down_gradient_sum + down_gradient
        query_total = query_total + up_query_grad
        value_total = value_total + up_value_grad
    return (outputs, backward_rows, parked_out, down_gradient_sum, query_total, value_total)
```

```python
import functools
import math

import jax
import jax.numpy as jnp
import numpy as np
from jax import lax
from jax.experimental import pallas as pl
from jax.experimental.pallas import tpu as pltpu
from jax.sharding import PartitionSpec as P

HEAD = 128
eps = 1e-05
rope_base = 500000.0
mask_fill = -1e30
BLOCK = 16
f32 = jnp.float32
bf16 = jnp.bfloat16


def rope_tables(row_count):
    half = HEAD // 2
    exponent = np.arange(half, dtype=np.float32) * np.float32(2.0 / HEAD)
    frequency = np.exp(-exponent * np.float32(math.log(rope_base)))
    angles = np.arange(row_count, dtype=np.float32)[:, None] * frequency[None, :]
    cosines, sines = np.cos(angles), np.sin(angles)
    return (
        np.concatenate([cosines, cosines], 1).astype(np.float32),
        np.concatenate([-sines, sines], 1).astype(np.float32),
    )


def dot(a, b):
    return jnp.dot(a, b, preferred_element_type=f32)


def dot_nt(a, b):
    return lax.dot_general(a, b, (((1,), (1,)), ((), ())), preferred_element_type=f32)


def dot_tn(a, b):
    return lax.dot_general(a, b, (((0,), (0,)), ((), ())), preferred_element_type=f32)


def cols(start, size):
    return pl.ds(pl.multiple_of(start, 128), size)


def loop(count, body):
    def step(i, carry):
        body(i)
        return carry

    lax.fori_loop(0, count, step, 0)


def kernel(
    sections,
    shares,
    gain,
    down,
    qup,
    vup,
    cos_ref,
    sin_ref,
    fids,
    bids,
    wq_hbm,
    wk_hbm,
    wv_hbm,
    wo_hbm,
    arriving,
    entering,
    returning,
    head_grad,
    parked,
    departing,
    returned,
    parked_out,
    g_down,
    g_query,
    g_value,
    wq,
    wk,
    wv,
    wo,
    x0,
    x1,
    p0,
    p1,
    c0,
    c1,
    nrm,
    rms,
    q,
    k,
    v,
    ctx,
    dctx,
    dk,
    dv,
    dn,
    part,
    recv,
    res,
    gd,
    gd_send,
    gd_recv,
    mask,
    w_sem,
    l_sem,
    gs_sem,
    gr_sem,
    cs_sem,
    cr_sem,
    hs_sem,
    hr_sem,
):
    rows, width = x0.shape
    share = width // shares
    dq_width = wq.shape[1]
    kv_width = wk.shape[1]
    groups = kv_width // HEAD
    per = dq_width // kv_width
    inverse = 1.0 / math.sqrt(HEAD)
    s = lax.axis_index("section")
    me = lax.axis_index("tensor")
    half = sections // 2
    mate = jnp.where(s < half, s + half, s - half)
    own = cols(me * share, share)
    q_step = min(512, dq_width)
    f_step = min(512, width)
    MESH = pl.DeviceIdType.MESH

    def peer(d):
        return lax.rem(me + d, shares)

    barrier = pltpu.get_barrier_semaphore()
    for d in range(1, shares):
        pl.semaphore_signal(barrier, inc=1, device_id=(s, peer(d)), device_id_type=MESH)
    pl.semaphore_signal(barrier, inc=1, device_id=(mate, me), device_id_type=MESH)

    for other in (lax.rem(s + 1, sections), lax.rem(s + sections - 1, sections)):
        pl.semaphore_signal(barrier, inc=1, device_id=(other, me), device_id_type=MESH)

    x0_local = pltpu.make_async_copy(arriving.at[0], x0.at[:, own], l_sem.at[0])
    c0_local = pltpu.make_async_copy(returning.at[0], c0.at[:, own], l_sem.at[1])
    x1_local = pltpu.make_async_copy(entering.at[0], x1.at[:, own], l_sem.at[2])
    c1_local = pltpu.make_async_copy(head_grad.at[0], c1.at[:, own], l_sem.at[3])
    x0_local.start()
    wk_copy = pltpu.make_async_copy(wk_hbm.at[0], wk, w_sem.at[0])
    wv_copy = pltpu.make_async_copy(wv_hbm.at[0], wv, w_sem.at[1])
    wk_copy.start()
    wv_copy.start()

    def wq_copy(i):
        piece = cols(i * q_step, q_step)
        return pltpu.make_async_copy(wq_hbm.at[0, :, piece], wq.at[:, piece], w_sem.at[2 + i])

    q_pieces = dq_width // q_step
    f_pieces = width // f_step

    def wo_copy(i):
        piece = cols(i * f_step, f_step)
        return pltpu.make_async_copy(
            wo_hbm.at[0, :, piece], wo.at[:, piece], w_sem.at[2 + q_pieces + i]
        )

    pl.semaphore_wait(barrier, shares + 2)

    def remote(source, target, send, receive, section, tensor):
        return pltpu.make_async_remote_copy(
            src_ref=source,
            dst_ref=target,
            send_sem=send,
            recv_sem=receive,
            device_id=(section, tensor),
            device_id_type=MESH,
        )

    def gather(source, buffer, slot):
        return [
            remote(
                source,
                buffer.at[:, own],
                gs_sem.at[slot, d - 1],
                gr_sem.at[slot, d - 1],
                s,
                peer(d),
            )
            for d in range(1, shares)
        ]

    def hop(source, target, slot, section):
        return remote(source, target, hs_sem.at[slot], hr_sem.at[slot], section, me)

    def start(copies):
        for copy in copies:
            copy.start()

    def wait(copies):
        for copy in copies:
            copy.wait()

    x0_gather = gather(arriving.at[0], x0, 0)
    c0_gather = gather(returning.at[0], c0, 1)
    x1_gather = gather(x1.at[:, own], x1, 2)
    c1_gather = gather(c1.at[:, own], c1, 3)
    p0_gather = gather(p0.at[:, own], p0, 4)
    p1_gather = gather(p1.at[:, own], p1, 5)
    p0_hop = hop(parked.at[0, 0], p0.at[:, own], 0, mate)
    p1_hop = hop(parked.at[0, 1], p1.at[:, own], 1, mate)
    s0_hop = hop(arriving.at[0], parked_out.at[0, 0], 2, mate)
    s1_hop = hop(x1.at[:, own], parked_out.at[0, 1], 3, mate)
    forth_hop = hop(res.at[0], x1.at[:, own], 4, lax.rem(s + 1, sections))
    back_hop = hop(res.at[1], c1.at[:, own], 5, lax.rem(s + sections - 1, sections))

    start(x0_gather)
    p0_hop.start()
    for i in range(q_pieces):
        wq_copy(i).start()
    for i in range(f_pieces):
        wo_copy(i).start()
    start(c0_gather)
    c0_local.start()

    @pl.when(s == 0)
    def _():
        x1_local.start()

    @pl.when(s == sections - 1)
    def _():
        c1_local.start()

    def rotate(value, direction):
        return value * cos_ref[...] + pltpu.roll(value, HEAD // 2, 1) * (
            sin_ref[...] * direction
        )

    def make_mask(ids, index):
        along = jnp.broadcast_to(ids[pl.ds(index, 1), :].astype(f32), (rows, rows))
        down_rows = along.T
        row = lax.broadcasted_iota(jnp.int32, (rows, rows), 0)
        column = lax.broadcasted_iota(jnp.int32, (rows, rows), 1)
        keep = (column <= row) & (along == down_rows)
        mask[...] = jnp.where(keep, 1, 0).astype(jnp.int32)

    def project(x, first):
        def norm(b):
            at = pl.ds(pl.multiple_of(b * BLOCK, BLOCK), BLOCK)
            value = x[at, :].astype(f32)
            r = lax.rsqrt(jnp.mean(value * value, axis=1, keepdims=True) + eps)
            rms[at, :] = jnp.broadcast_to(r, (BLOCK, HEAD))
            nrm[at, :] = (value * r * gain[...]).astype(bf16)

        loop(rows // BLOCK, norm)
        low = dot_nt(nrm[...], down[...]).astype(bf16)
        if first:
            wk_copy.wait()

        kv_step = min(256, kv_width)

        def keys(i):
            out = dot(nrm[...], wk[:, cols(i * kv_step, kv_step)])
            for j in range(kv_step // HEAD):
                k[:, cols(i * kv_step + j * HEAD, HEAD)] = rotate(
                    out[:, j * HEAD : (j + 1) * HEAD], 1.0
                ).astype(bf16)

        loop(kv_width // kv_step, keys)
        if first:
            wv_copy.wait()

        def values(i):
            at = cols(i * kv_step, kv_step)
            v[:, at] = (dot(nrm[...], wv[:, at]) + dot(low, vup[:, at])).astype(bf16)

        loop(kv_width // kv_step, values)

        def queries(i):
            if first:
                wq_copy(i).wait()
            at = cols(i * q_step, q_step)
            out = dot(nrm[...], wq[:, at]) + dot(low, qup[:, at])
            for j in range(q_step // HEAD):
                q[:, cols(i * q_step + j * HEAD, HEAD)] = rotate(
                    out[:, j * HEAD : (j + 1) * HEAD], 1.0
                ).astype(bf16)

        loop(q_pieces, queries)

    def stack(ref, g):
        return jnp.concatenate(
            [ref[:, cols((g * per + j) * HEAD, HEAD)] for j in range(per)], axis=0
        )

    def softmax(q4, kk):
        scores = dot_nt(q4, kk) * inverse
        allowed = jnp.concatenate([mask[...]] * per, axis=0)
        scores = jnp.where(allowed > 0, scores, mask_fill)
        weights = jnp.exp(scores - jnp.max(scores, axis=1, keepdims=True))
        return weights / jnp.sum(weights, axis=1, keepdims=True)

    def exchange(base, target, slot):
        copies = [
            remote(
                part.at[:, cols(peer(d) * share, share)],
                recv.at[slot, d - 1],
                cs_sem.at[slot, d - 1],
                cr_sem.at[slot, d - 1],
                s,
                peer(d),
            )
            for d in range(1, shares)
        ]
        start(copies)
        wait(copies)

        def add(b):
            at = pl.ds(pl.multiple_of(b * BLOCK, BLOCK), BLOCK)
            total = part[at, own].astype(f32)
            for d in range(1, shares):
                total = total + recv[slot, d - 1, at, :].astype(f32)
            target[at, :] = (base[at, own].astype(f32) + total).astype(bf16)

        loop(rows // BLOCK, add)

    def forward(x, ids, index, target, slot, first):
        make_mask(ids, index)
        project(x, first)

        def attend(g):
            probs = softmax(stack(q, g), k[:, cols(g * HEAD, HEAD)])
            out = dot(probs.astype(bf16), v[:, cols(g * HEAD, HEAD)]).astype(bf16)
            for j in range(per):
                ctx[:, cols((g * per + j) * HEAD, HEAD)] = out[j * rows : (j + 1) * rows]

        loop(groups, attend)

        def output(i):
            if first:
                wo_copy(i).wait()
            at = cols(i * f_step, f_step)
            part[:, at] = dot(ctx[...], wo[:, at]).astype(bf16)

        loop(f_pieces, output)
        exchange(x, target, slot)

    def backward(x, c, ids, index, target, slot, first):
        make_mask(ids, index)
        project(x, False)
        low_t = dot_nt(down[...], nrm[...]).astype(bf16)

        c_step = min(512, dq_width)

        def contexts(i):
            at = cols(i * c_step, c_step)
            dctx[:, at] = dot_nt(c[...], wo[at, :]).astype(bf16)

        loop(dq_width // c_step, contexts)

        def attend(g):
            at = cols(g * HEAD, HEAD)
            q4, kk, dc4 = stack(q, g), k[:, at], stack(dctx, g)
            probs = softmax(q4, kk)
            d_probs = dot_nt(dc4, v[:, at])
            dv[:, at] = dot_tn(probs.astype(bf16), dc4).astype(bf16)
            d_score = (
                probs * (d_probs - jnp.sum(d_probs * probs, axis=1, keepdims=True)) * inverse
            ).astype(bf16)
            dq4 = dot(d_score, kk)
            dk[:, at] = rotate(dot_tn(d_score, q4), -1.0).astype(bf16)
            for j in range(per):
                ctx[:, cols((g * per + j) * HEAD, HEAD)] = rotate(
                    dq4[j * rows : (j + 1) * rows], -1.0
                ).astype(bf16)

        loop(groups, attend)
        d_low = (dot_nt(ctx[...], qup[...]) + dot_nt(dv[...], vup[...])).astype(bf16)
        d_low_t = (dot_nt(qup[...], ctx[...]) + dot_nt(vup[...], dv[...])).astype(bf16)

        def normed(i):
            at = cols(i * f_step, f_step)
            dn[:, at] = (
                dot_nt(ctx[...], wq[at, :])
                + dot_nt(dk[...], wk[at, :])
                + dot_nt(dv[...], wv[at, :])
                + dot(d_low, down[:, at])
            )

        loop(f_pieces, normed)

        def inputs(b):
            at = pl.ds(pl.multiple_of(b * BLOCK, BLOCK), BLOCK)
            r = rms[at, 0:1]
            weighted = dn[at, :] * gain[...]
            value = x[at, :].astype(f32)
            mean = jnp.mean(value * weighted, axis=1, keepdims=True)
            part[at, :] = (r * weighted - value * (r * r * r * mean)).astype(bf16)

        loop(rows // BLOCK, inputs)
        exchange(c, target, slot)

        rank = g_query.shape[1]
        up_q = dot(low_t, ctx[...])[:rank]
        up_v = dot(low_t, dv[...])[rank:]
        g_query[0] = up_q if first else g_query[0] + up_q
        g_value[0] = up_v if first else g_value[0] + up_v

        def downs(i):
            at = cols(i * f_step, f_step)
            value = dot(d_low_t, nrm[:, at])
            gd[:, at] = value if first else gd[:, at] + value

        return functools.partial(loop, f_pieces, downs)

    x0_local.wait()
    wait(x0_gather)
    forward(x0, fids, sections - 1 - s, res.at[0], 0, True)

    @pl.when(s < sections - 1)
    def _():
        forth_hop.start()

    p0_hop.wait()
    p1_hop.start()
    s0_hop.start()
    start(p0_gather)
    c0_local.wait()
    wait(c0_gather)
    wait(p0_gather)

    backward(p0, c0, bids, s, res.at[1], 2, True)()

    @pl.when(s > 0)
    def _():
        back_hop.start()
        forth_hop.wait_recv()

    @pl.when(s == 0)
    def _():
        x1_local.wait()

    start(x1_gather)
    s1_hop.start()
    wait(x1_gather)

    forward(x1, fids, sections - s, departing.at[0], 1, False)

    p1_hop.wait()
    start(p1_gather)

    @pl.when(s < sections - 1)
    def _():
        back_hop.wait_recv()

    @pl.when(s == sections - 1)
    def _():
        c1_local.wait()

    start(c1_gather)
    wait(p1_gather)
    wait(c1_gather)

    backward(p1, c1, bids, s + 1, returned.at[0], 3, False)()

    gd_send[...] = gd[...].astype(bf16)
    copies = [
        remote(
            gd_send.at[:, cols(peer(d) * share, share)],
            gd_recv.at[d - 1],
            gs_sem.at[6, d - 1],
            gr_sem.at[6, d - 1],
            s,
            peer(d),
        )
        for d in range(1, shares)
    ]
    start(copies)
    wait(copies)
    total = gd[:, own]
    for d in range(1, shares):
        total = total + gd_recv[d - 1].astype(f32)
    rank = g_query.shape[1]
    g_down[0, 0] = total[:rank]
    g_down[0, 1] = total[rank:]

    @pl.when(s < sections - 1)
    def _():
        forth_hop.wait_send()

    @pl.when(s > 0)
    def _():
        back_hop.wait_send()

    s0_hop.wait()
    s1_hop.wait()


def per_device(
    gain, wq, wk, wv, wo, down, qup, vup, arriving, entering, returning, head_grad, parked,
    fids, bids,
):
    sections = lax.axis_size("section")
    shares = lax.axis_size("tensor")
    rows, share = arriving.shape[1:]
    width = share * shares
    dq_width, kv_width = wq.shape[2], wk.shape[2]
    rank = qup.shape[1]
    cosines, sines = rope_tables(rows)
    zeros_q, zeros_v = jnp.zeros_like(qup[0]), jnp.zeros_like(vup[0])
    qup_wide = jnp.concatenate([qup[0], zeros_q], axis=0)
    vup_wide = jnp.concatenate([zeros_v, vup[0]], axis=0)
    down_flat = down.reshape(2 * rank, width)
    vmem = pl.BlockSpec(memory_space=pltpu.VMEM)
    anywhere = pl.BlockSpec(memory_space=pl.ANY)
    others = max(shares - 1, 1)
    pieces = 2 + dq_width // min(512, dq_width) + width // min(512, width)
    act = pltpu.VMEM((rows, width), bf16)
    return pl.pallas_call(
        functools.partial(kernel, sections, shares),
        out_shape=(
            jax.ShapeDtypeStruct((1, rows, share), bf16),
            jax.ShapeDtypeStruct((1, rows, share), bf16),
            jax.ShapeDtypeStruct(parked.shape, bf16),
            jax.ShapeDtypeStruct((1, 2, rank, share), f32),
            jax.ShapeDtypeStruct((1, rank, dq_width), f32),
            jax.ShapeDtypeStruct((1, rank, kv_width), f32),
        ),
        in_specs=[vmem] * 8 + [anywhere] * 9,
        out_specs=(vmem, vmem, anywhere, vmem, vmem, vmem),
        scratch_shapes=[
            pltpu.VMEM(wq.shape[1:], bf16),
            pltpu.VMEM(wk.shape[1:], bf16),
            pltpu.VMEM(wv.shape[1:], bf16),
            pltpu.VMEM(wo.shape[1:], bf16),
            act, act, act, act, act, act,
            act,
            pltpu.VMEM((rows, HEAD), f32),
            pltpu.VMEM((rows, dq_width), bf16),
            pltpu.VMEM((rows, kv_width), bf16),
            pltpu.VMEM((rows, kv_width), bf16),
            pltpu.VMEM((rows, dq_width), bf16),
            pltpu.VMEM((rows, dq_width), bf16),
            pltpu.VMEM((rows, kv_width), bf16),
            pltpu.VMEM((rows, kv_width), bf16),
            pltpu.VMEM((rows, width), f32),
            act,
            pltpu.VMEM((4, others, rows, share), bf16),
            pltpu.VMEM((2, rows, share), bf16),
            pltpu.VMEM((2 * rank, width), f32),
            pltpu.VMEM((2 * rank, width), bf16),
            pltpu.VMEM((others, 2 * rank, share), bf16),
            pltpu.VMEM((rows, rows), jnp.int32),
            pltpu.SemaphoreType.DMA((pieces,)),
            pltpu.SemaphoreType.DMA((4,)),
            pltpu.SemaphoreType.DMA((7, others)),
            pltpu.SemaphoreType.DMA((7, others)),
            pltpu.SemaphoreType.DMA((4, others)),
            pltpu.SemaphoreType.DMA((4, others)),
            pltpu.SemaphoreType.DMA((6,)),
            pltpu.SemaphoreType.DMA((6,)),
        ],
        compiler_params=pltpu.CompilerParams(
            collective_id=0, has_side_effects=True, vmem_limit_bytes=63 * 2**20
        ),
    )(
        gain, down_flat, qup_wide, vup_wide, jnp.asarray(cosines), jnp.asarray(sines),
        fids, bids, wq, wk, wv, wo, arriving, entering, returning, head_grad, parked,
    )


def solution(mesh):
    by_share = P("section", None, "tensor")
    placed = (
        P("section", None), by_share, by_share, by_share,
        P("section", "tensor", None), P("section", None, None, None), by_share, by_share,
        by_share, P(None, None, "tensor"), by_share, P(None, None, "tensor"),
        P("section", None, None, "tensor"), P(), P(),
    )
    return jax.shard_map(
        per_device,
        mesh=mesh,
        in_specs=placed,
        out_specs=(
            by_share, by_share, P("section", None, None, "tensor"),
            P("section", None, None, "tensor"), by_share, by_share,
        ),
        check_vma=False,
    )
```

```python
import functools
import math

import jax
import jax.numpy as jnp
import numpy as np
from jax import lax
from jax.experimental import pallas as pl
from jax.experimental.pallas import tpu as pltpu
from jax.sharding import PartitionSpec as P

HEAD = 128
eps = 1e-05
rope_base = 500000.0
mask_fill = -1e30
BLOCK = 16
f32 = jnp.float32
bf16 = jnp.bfloat16


def rope_tables(row_count):
    half = HEAD // 2
    exponent = np.arange(half, dtype=np.float32) * np.float32(2.0 / HEAD)
    frequency = np.exp(-exponent * np.float32(math.log(rope_base)))
    angles = np.arange(row_count, dtype=np.float32)[:, None] * frequency[None, :]
    cosines, sines = np.cos(angles), np.sin(angles)
    return (
        np.concatenate([cosines, cosines], 1).astype(np.float32),
        np.concatenate([-sines, sines], 1).astype(np.float32),
    )


def dot(a, b):
    return jnp.dot(a, b, preferred_element_type=f32)


def dot_nt(a, b):
    return lax.dot_general(a, b, (((1,), (1,)), ((), ())), preferred_element_type=f32)


def dot_tn(a, b):
    return lax.dot_general(a, b, (((0,), (0,)), ((), ())), preferred_element_type=f32)


def cols(start, size):
    return pl.ds(pl.multiple_of(start, 128), size)


def loop(count, body):
    def step(i, carry):
        body(i)
        return carry

    lax.fori_loop(0, count, step, 0)


def kernel(
    sections,
    shares,
    gain,
    down,
    qup_in,
    vup_in,
    cos_ref,
    sin_ref,
    fids,
    bids,
    wq_hbm,
    wk_hbm,
    wv_hbm,
    wo_hbm,
    arriving,
    entering,
    returning,
    head_grad,
    parked,
    departing,
    returned,
    parked_out,
    g_down,
    g_query,
    g_value,
    wq,
    wk,
    wv,
    wo,
    x0,
    x1,
    p0,
    p1,
    c0,
    c1,
    nrm,
    rms,
    q,
    k,
    v,
    ctx,
    dctx,
    dk,
    dv,
    dn,
    part,
    recv,
    res,
    gd,
    gd_send,
    gd_recv,
    mask,
    qup,
    vup,
    w_sem,
    l_sem,
    gs_sem,
    gr_sem,
    cs_sem,
    cr_sem,
    hs_sem,
    hr_sem,
):
    rows, width = x0.shape
    share = width // shares
    dq_width = wq.shape[1]
    kv_width = wk.shape[1]
    groups = kv_width // HEAD
    per = dq_width // kv_width
    inverse = 1.0 / math.sqrt(HEAD)
    s = lax.axis_index("section")
    me = lax.axis_index("tensor")
    half = sections // 2
    mate = jnp.where(s < half, s + half, s - half)
    own = cols(me * share, share)
    q_step = min(512, dq_width)
    f_step = min(512, share)
    MESH = pl.DeviceIdType.MESH

    def peer(d):
        return lax.rem(me + d, shares)

    barrier = pltpu.get_barrier_semaphore()
    for d in range(1, shares):
        pl.semaphore_signal(barrier, inc=1, device_id=(s, peer(d)), device_id_type=MESH)
    pl.semaphore_signal(barrier, inc=1, device_id=(mate, me), device_id_type=MESH)

    for other in (lax.rem(s + 1, sections), lax.rem(s + sections - 1, sections)):
        pl.semaphore_signal(barrier, inc=1, device_id=(other, me), device_id_type=MESH)

    x0_local = pltpu.make_async_copy(arriving.at[0], x0.at[:, own], l_sem.at[0])
    c0_local = pltpu.make_async_copy(returning.at[0], c0.at[:, own], l_sem.at[1])
    x1_local = pltpu.make_async_copy(entering.at[0], x1.at[:, own], l_sem.at[2])
    c1_local = pltpu.make_async_copy(head_grad.at[0], c1.at[:, own], l_sem.at[3])
    x0_local.start()
    wk_copy = pltpu.make_async_copy(wk_hbm.at[0], wk, w_sem.at[0])
    wv_copy = pltpu.make_async_copy(wv_hbm.at[0], wv, w_sem.at[1])
    wk_copy.start()
    wv_copy.start()

    def wq_copy(i):
        piece = cols(i * q_step, q_step)
        return pltpu.make_async_copy(wq_hbm.at[0, :, piece], wq.at[:, piece], w_sem.at[2 + i])

    q_pieces = dq_width // q_step
    f_pieces = width // f_step

    def wo_copy(i):
        piece = cols(i * f_step, f_step)
        return pltpu.make_async_copy(
            wo_hbm.at[0, :, piece], wo.at[:, piece], w_sem.at[2 + q_pieces + i]
        )

    pl.semaphore_wait(barrier, shares + 2)

    def remote(source, target, send, receive, section, tensor):
        return pltpu.make_async_remote_copy(
            src_ref=source,
            dst_ref=target,
            send_sem=send,
            recv_sem=receive,
            device_id=(section, tensor),
            device_id_type=MESH,
        )

    def gather(source, buffer, slot):
        return [
            remote(
                source,
                buffer.at[:, own],
                gs_sem.at[slot, d - 1],
                gr_sem.at[slot, d - 1],
                s,
                peer(d),
            )
            for d in range(1, shares)
        ]

    def hop(source, target, slot, section):
        return remote(source, target, hs_sem.at[slot], hr_sem.at[slot], section, me)

    def start(copies):
        for copy in copies:
            copy.start()

    def wait(copies):
        for copy in copies:
            copy.wait()

    x0_gather = gather(arriving.at[0], x0, 0)
    c0_gather = gather(returning.at[0], c0, 1)
    x1_gather = gather(x1.at[:, own], x1, 2)
    c1_gather = gather(c1.at[:, own], c1, 3)
    p0_gather = gather(p0.at[:, own], p0, 4)
    p1_gather = gather(p1.at[:, own], p1, 5)
    p0_hop = hop(parked.at[0, 0], p0.at[:, own], 0, mate)
    p1_hop = hop(parked.at[0, 1], p1.at[:, own], 1, mate)
    s0_hop = hop(arriving.at[0], parked_out.at[0, 0], 2, mate)
    s1_hop = hop(x1.at[:, own], parked_out.at[0, 1], 3, mate)
    forth_hop = hop(res.at[0], x1.at[:, own], 4, lax.rem(s + 1, sections))
    back_hop = hop(res.at[1], c1.at[:, own], 5, lax.rem(s + sections - 1, sections))

    start(x0_gather)
    p0_hop.start()
    for i in range(q_pieces):
        wq_copy(i).start()
    for i in range(f_pieces):
        wo_copy(i).start()
    start(c0_gather)
    c0_local.start()
    up_q_rows, up_v_rows = qup_in[0].astype(f32), vup_in[0].astype(f32)
    qup[...] = jnp.concatenate([up_q_rows, jnp.zeros_like(up_q_rows)], axis=0).astype(bf16)
    vup[...] = jnp.concatenate([jnp.zeros_like(up_v_rows), up_v_rows], axis=0).astype(bf16)

    @pl.when(s == 0)
    def _():
        x1_local.start()

    @pl.when(s == sections - 1)
    def _():
        c1_local.start()

    def rotate(value, direction):
        return value * cos_ref[...] + pltpu.roll(value, HEAD // 2, 1) * (
            sin_ref[...] * direction
        )

    def make_mask(ids, index):
        along = jnp.broadcast_to(ids[pl.ds(index, 1), :].astype(f32), (rows, rows))
        down_rows = along.T
        row = lax.broadcasted_iota(jnp.int32, (rows, rows), 0)
        column = lax.broadcasted_iota(jnp.int32, (rows, rows), 1)
        keep = (column <= row) & (along == down_rows)
        mask[...] = jnp.where(keep, 1, 0).astype(jnp.int32)

    def project(x, first):
        def norm(b):
            at = pl.ds(pl.multiple_of(b * BLOCK, BLOCK), BLOCK)
            value = x[at, :].astype(f32)
            r = lax.rsqrt(jnp.mean(value * value, axis=1, keepdims=True) + eps)
            rms[at, :] = jnp.broadcast_to(r, (BLOCK, HEAD))
            nrm[at, :] = (value * r * gain[...]).astype(bf16)

        loop(rows // BLOCK, norm)
        low = dot_nt(nrm[...], down[...]).astype(bf16)
        if first:
            wk_copy.wait()

        kv_step = min(256, kv_width)

        def keys(i):
            out = dot(nrm[...], wk[:, cols(i * kv_step, kv_step)])
            for j in range(kv_step // HEAD):
                k[:, cols(i * kv_step + j * HEAD, HEAD)] = rotate(
                    out[:, j * HEAD : (j + 1) * HEAD], 1.0
                ).astype(bf16)

        loop(kv_width // kv_step, keys)
        if first:
            wv_copy.wait()

        def values(i):
            at = cols(i * kv_step, kv_step)
            v[:, at] = (dot(nrm[...], wv[:, at]) + dot(low, vup[:, at])).astype(bf16)

        loop(kv_width // kv_step, values)

        def queries(i):
            if first:
                wq_copy(i).wait()
            at = cols(i * q_step, q_step)
            out = dot(nrm[...], wq[:, at]) + dot(low, qup[:, at])
            for j in range(q_step // HEAD):
                q[:, cols(i * q_step + j * HEAD, HEAD)] = rotate(
                    out[:, j * HEAD : (j + 1) * HEAD], 1.0
                ).astype(bf16)

        loop(q_pieces, queries)

    def stack(ref, g):
        return jnp.concatenate(
            [ref[:, cols((g * per + j) * HEAD, HEAD)] for j in range(per)], axis=0
        )

    def softmax(q4, kk):
        scores = dot_nt(q4, kk) * inverse
        allowed = jnp.concatenate([mask[...]] * per, axis=0)
        scores = jnp.where(allowed > 0, scores, mask_fill)
        weights = jnp.exp(scores - jnp.max(scores, axis=1, keepdims=True))
        return weights / jnp.sum(weights, axis=1, keepdims=True)

    def sends(slot):
        return [
            remote(
                part.at[:, cols(peer(d) * share, share)],
                recv.at[slot, d - 1],
                cs_sem.at[slot, d - 1],
                cr_sem.at[slot, d - 1],
                s,
                peer(d),
            )
            for d in range(1, shares)
        ]

    def merge(base, target, slot, copies):
        wait(copies)

        def add(b):
            at = pl.ds(pl.multiple_of(b * BLOCK, BLOCK), BLOCK)
            total = part[at, own].astype(f32)
            for d in range(1, shares):
                total = total + recv[slot, d - 1, at, :].astype(f32)
            target[at, :] = (base[at, own].astype(f32) + total).astype(bf16)

        loop(rows // BLOCK, add)

    def forward(x, ids, index, target, slot, first, between):
        make_mask(ids, index)
        project(x, first)

        def attend(g):
            probs = softmax(stack(q, g), k[:, cols(g * HEAD, HEAD)])
            out = dot(probs.astype(bf16), v[:, cols(g * HEAD, HEAD)]).astype(bf16)
            for j in range(per):
                ctx[:, cols((g * per + j) * HEAD, HEAD)] = out[j * rows : (j + 1) * rows]

        loop(groups, attend)
        between()

        copies = sends(slot)
        for d in range(1, shares + 1):

            def output(i):
                piece = peer(d) * (share // f_step) + i
                if first:
                    wo_copy(piece).wait()
                at = cols(piece * f_step, f_step)
                part[:, at] = dot(ctx[...], wo[:, at]).astype(bf16)

            loop(share // f_step, output)
            if d < shares:
                copies[d - 1].start()
        merge(x, target, slot, copies)

    def backward(x, c, ids, index, target, slot, first, arrive, between):
        make_mask(ids, index)
        c_step = min(512, dq_width)

        def contexts(i):
            at = cols(i * c_step, c_step)
            dctx[:, at] = dot_nt(c[...], wo[at, :]).astype(bf16)

        pieces = dq_width // c_step
        early = pieces // 2
        loop(early, contexts)
        arrive()
        loop(pieces - early, lambda i: contexts(early + i))
        wait(p0_gather if first else p1_gather)
        project(x, False)
        low_t = dot_nt(down[...], nrm[...]).astype(bf16)

        def attend(g):
            at = cols(g * HEAD, HEAD)
            q4, kk, dc4 = stack(q, g), k[:, at], stack(dctx, g)
            probs = softmax(q4, kk)
            d_probs = dot_nt(dc4, v[:, at])
            dv[:, at] = dot_tn(probs.astype(bf16), dc4).astype(bf16)
            d_score = (
                probs * (d_probs - jnp.sum(d_probs * probs, axis=1, keepdims=True)) * inverse
            ).astype(bf16)
            dq4 = dot(d_score, kk)
            dk[:, at] = rotate(dot_tn(d_score, q4), -1.0).astype(bf16)
            for j in range(per):
                ctx[:, cols((g * per + j) * HEAD, HEAD)] = rotate(
                    dq4[j * rows : (j + 1) * rows], -1.0
                ).astype(bf16)

        loop(groups, attend)
        between()
        d_low = (dot_nt(ctx[...], qup[...]) + dot_nt(dv[...], vup[...])).astype(bf16)
        d_low_t = (dot_nt(qup[...], ctx[...]) + dot_nt(vup[...], dv[...])).astype(bf16)

        def normed(i):
            at = cols(i * f_step, f_step)
            dn[:, at] = (
                dot_nt(ctx[...], wq[at, :])
                + dot_nt(dk[...], wk[at, :])
                + dot_nt(dv[...], wv[at, :])
                + dot(d_low, down[:, at])
            )

        loop(f_pieces, normed)

        def inputs(b):
            at = pl.ds(pl.multiple_of(b * BLOCK, BLOCK), BLOCK)
            r = rms[at, 0:1]
            weighted = dn[at, :] * gain[...]
            value = x[at, :].astype(f32)
            mean = jnp.mean(value * weighted, axis=1, keepdims=True)
            part[at, :] = (r * weighted - value * (r * r * r * mean)).astype(bf16)

        loop(rows // BLOCK, inputs)
        copies = sends(slot)
        start(copies)

        rank = g_query.shape[1]
        up_q = dot(low_t, ctx[...])[:rank]
        up_v = dot(low_t, dv[...])[rank:]
        g_query[0] = up_q if first else g_query[0] + up_q
        g_value[0] = up_v if first else g_value[0] + up_v

        def downs(i):
            at = cols(i * f_step, f_step)
            value = dot(d_low_t, nrm[:, at])
            gd[:, at] = value if first else gd[:, at] + value

        loop(f_pieces, downs)
        merge(c, target, slot, copies)

    x0_local.wait()
    wait(x0_gather)
    forward(x0, fids, sections - 1 - s, res.at[0], 0, True, lambda: None)

    @pl.when(s < sections - 1)
    def _():
        forth_hop.start()

    def stored_first():
        p0_hop.wait()
        p1_hop.start()
        start(p0_gather)

    def next_input():
        @pl.when(s > 0)
        def _():
            forth_hop.wait_recv()

        @pl.when(s == 0)
        def _():
            x1_local.wait()

        start(x1_gather)
        s0_hop.start()

    c0_local.wait()
    wait(c0_gather)
    backward(p0, c0, bids, s, res.at[1], 2, True, stored_first, next_input)

    @pl.when(s > 0)
    def _():
        back_hop.start()

    def next_cotangent():
        @pl.when(s < sections - 1)
        def _():
            back_hop.wait_recv()

        @pl.when(s == sections - 1)
        def _():
            c1_local.wait()

        start(c1_gather)
        p1_hop.wait()
        start(p1_gather)
        s1_hop.start()

    wait(x1_gather)
    forward(x1, fids, sections - s, departing.at[0], 1, False, next_cotangent)

    wait(c1_gather)
    backward(p1, c1, bids, s + 1, returned.at[0], 3, False, lambda: None, lambda: None)

    gd_send[...] = gd[...].astype(bf16)
    copies = [
        remote(
            gd_send.at[:, cols(peer(d) * share, share)],
            gd_recv.at[d - 1],
            gs_sem.at[6, d - 1],
            gr_sem.at[6, d - 1],
            s,
            peer(d),
        )
        for d in range(1, shares)
    ]
    start(copies)
    wait(copies)
    total = gd[:, own]
    for d in range(1, shares):
        total = total + gd_recv[d - 1].astype(f32)
    rank = g_query.shape[1]
    g_down[0, 0] = total[:rank]
    g_down[0, 1] = total[rank:]

    @pl.when(s < sections - 1)
    def _():
        forth_hop.wait_send()

    @pl.when(s > 0)
    def _():
        back_hop.wait_send()

    s0_hop.wait()
    s1_hop.wait()


def hand_on(count, *refs):
    sems = refs[2 * count]
    copies = [
        pltpu.make_async_copy(refs[i], refs[count + i], sems.at[i]) for i in range(count)
    ]
    for copy in copies:
        copy.start()
    for copy in copies:
        copy.wait()


def per_device(
    gain, wq, wk, wv, wo, down, qup, vup, arriving, entering, returning, head_grad, parked,
    fids, bids,
):
    sections = lax.axis_size("section")
    shares = lax.axis_size("tensor")
    rows, share = arriving.shape[1:]
    width = share * shares
    dq_width, kv_width = wq.shape[2], wk.shape[2]
    rank = qup.shape[1]
    cosines, sines = rope_tables(rows)
    down_flat = down.reshape(2 * rank, width)
    vmem = pl.BlockSpec(memory_space=pltpu.VMEM)
    anywhere = pl.BlockSpec(memory_space=pl.ANY)
    others = max(shares - 1, 1)
    pieces = 2 + dq_width // min(512, dq_width) + width // min(512, share)
    act = pltpu.VMEM((rows, width), bf16)
    outs = pl.pallas_call(
        functools.partial(kernel, sections, shares),
        out_shape=(
            jax.ShapeDtypeStruct((1, rows, share), bf16),
            jax.ShapeDtypeStruct((1, rows, share), bf16),
            jax.ShapeDtypeStruct(parked.shape, bf16),
            jax.ShapeDtypeStruct((1, 2, rank, share), f32),
            jax.ShapeDtypeStruct((1, rank, dq_width), f32),
            jax.ShapeDtypeStruct((1, rank, kv_width), f32),
        ),
        in_specs=[vmem] * 8 + [anywhere] * 9,
        out_specs=(vmem, vmem, anywhere, vmem, vmem, vmem),
        scratch_shapes=[
            pltpu.VMEM(wq.shape[1:], bf16),
            pltpu.VMEM(wk.shape[1:], bf16),
            pltpu.VMEM(wv.shape[1:], bf16),
            pltpu.VMEM(wo.shape[1:], bf16),
            act, act, act, act, act, act,
            act,
            pltpu.VMEM((rows, HEAD), f32),
            pltpu.VMEM((rows, dq_width), bf16),
            pltpu.VMEM((rows, kv_width), bf16),
            pltpu.VMEM((rows, kv_width), bf16),
            pltpu.VMEM((rows, dq_width), bf16),
            pltpu.VMEM((rows, dq_width), bf16),
            pltpu.VMEM((rows, kv_width), bf16),
            pltpu.VMEM((rows, kv_width), bf16),
            pltpu.VMEM((rows, width), f32),
            act,
            pltpu.VMEM((4, others, rows, share), bf16),
            pltpu.VMEM((2, rows, share), bf16),
            pltpu.VMEM((2 * rank, width), f32),
            pltpu.VMEM((2 * rank, width), bf16),
            pltpu.VMEM((others, 2 * rank, share), bf16),
            pltpu.VMEM((rows, rows), jnp.int32),
            pltpu.VMEM((2 * rank, dq_width), bf16),
            pltpu.VMEM((2 * rank, kv_width), bf16),
            pltpu.SemaphoreType.DMA((pieces,)),
            pltpu.SemaphoreType.DMA((4,)),
            pltpu.SemaphoreType.DMA((7, others)),
            pltpu.SemaphoreType.DMA((7, others)),
            pltpu.SemaphoreType.DMA((4, others)),
            pltpu.SemaphoreType.DMA((4, others)),
            pltpu.SemaphoreType.DMA((6,)),
            pltpu.SemaphoreType.DMA((6,)),
        ],
        compiler_params=pltpu.CompilerParams(
            collective_id=0, has_side_effects=True, vmem_limit_bytes=63 * 2**20
        ),
    )(
        gain, down_flat, qup, vup, jnp.asarray(cosines), jnp.asarray(sines),
        fids, bids, wq, wk, wv, wo, arriving, entering, returning, head_grad, parked,
    )
    return pl.pallas_call(
        functools.partial(hand_on, len(outs)),
        out_shape=tuple(jax.ShapeDtypeStruct(o.shape, o.dtype) for o in outs),
        in_specs=[anywhere] * len(outs),
        out_specs=(anywhere,) * len(outs),
        scratch_shapes=[pltpu.SemaphoreType.DMA((len(outs),))],
    )(*outs)


def solution(mesh):
    by_share = P("section", None, "tensor")
    placed = (
        P("section", None), by_share, by_share, by_share,
        P("section", "tensor", None), P("section", None, None, None), by_share, by_share,
        by_share, P(None, None, "tensor"), by_share, P(None, None, "tensor"),
        P("section", None, None, "tensor"), P(), P(),
    )
    return jax.shard_map(
        per_device,
        mesh=mesh,
        in_specs=placed,
        out_specs=(
            by_share, by_share, P("section", None, None, "tensor"),
            P("section", None, None, "tensor"), by_share, by_share,
        ),
        check_vma=False,
    )
```
